32 devices in a mesh: sec: 2 (over x), grp: 16 (over z, y, core), tp: 1.
Axes of the slice: x: 2, y: 2, z: 4, core: 2. Of those that a mesh axis runs over, the one named last changes fastest.
Arguments:
- hidden_in: bfloat16 [128, 7168], P(('sec', 'grp', 'tp')), may hold values from -6 to 6
- queries: bfloat16 [128, 128, 1, 576], P(('sec', 'grp'), None, 'tp'), may hold values from -61 to 61
- latent_cache: bfloat16 [128, 64, 576], P(('sec', 'grp')), may hold values from -6 to 6
- lengths: int32 [128], P(('sec', 'grp')), may hold values from 2 to 64, as said below
- w_uv: bfloat16 [128, 1, 512, 128], P(None, 'tp'), may hold values from -0.75 to 0.75
- attn_weight: bfloat16 [128, 1, 128, 7168], P(None, 'tp', None, 'grp'), may hold values from -0.046875 to 0.046875
- norm_gain: float32 [7168], replicated, may hold values from 0.1 to 1.9
- router: bfloat16 [7168, 32], replicated, may hold values from -0.0625 to 0.0625
- routes: int32 [128, 8], P(('sec', 'grp', 'tp')), may hold values from 0 to 31, all different within a row; in each aligned block of 4 rows (0 to 3, 4 to 7, ...) at most 2 rows name the same one
- live_counts: int32 [32], P(('sec', 'grp', 'tp')), may hold values from 3 to 4, as said below
- expert_in: bfloat16 [32, 7168, 2, 1024], P(('sec', 'grp'), None, None, 'tp'), may hold values from -0.0625 to 0.0625
- expert_out: bfloat16 [32, 1024, 7168], P(('sec', 'grp'), 'tp'), may hold values from -0.5 to 0.5
Outputs:
- layer_out: bfloat16 [128, 7168], P(('sec', 'grp', 'tp'))
The draws below stay inside these ranges and needn't reach their ends.
Inputs may be any that keep to these rules, and one draw needn't show every extreme that they name: `lengths`: some request has exactly 64 cached positions and some has 2. `live_counts`: some device has all 4 slots live and some has exactly 3. `routes`: the 8 experts of a token differ. Within the rows of one device (aligned blocks of 4 rows) no expert is named by more than 2 rows, a bound that some block reaches.
All inputs are finite; a program needn't handle non-finite values.
Results may differ from the reference program's by a relative error of at most 0.018.
Values may be sent and summed in bfloat16 or wider, within the bound.
A program may use at most 192 MiB of HBM per device.

```python
import math
import jax
import jax.numpy as jnp
import numpy as np
from jax import lax

D = 7168
HEADS = 128
KV_RANK = 512
V_DIM = 128
HID = 1024
TOKENS_PER_UNIT = 4
CACHE_LEN = 64
QK_DIM = 576
HEAD_BLOCK = 128
TOKENS = 128
EXPERTS = 32
TOPK = 8
MOST = 2
N_TP = 1


def draw_queries(key, part):
    shape = (TOKENS, HEAD_BLOCK, HEADS // HEAD_BLOCK, QK_DIM)
    query_key = jax.random.fold_in(key, 1)
    values = jnp.clip(jax.random.normal(query_key, shape, jnp.float32), -6.0, 6.0)
    return values.astype(jnp.bfloat16)


def draw_latent_cache(key, part):
    shape = (TOKENS, CACHE_LEN, QK_DIM)
    cache_key = jax.random.fold_in(key, 2)
    values = jnp.clip(jax.random.normal(cache_key, shape, jnp.float32), -6.0, 6.0)
    return values.astype(jnp.bfloat16)


def draw_lengths(key, part):
    drawn = jax.random.randint(jax.random.fold_in(key, 11), (TOKENS,), 2, CACHE_LEN + 1)
    longest = jax.random.randint(jax.random.fold_in(key, 12), (), 0, TOKENS)
    shortest = (longest + 1 + jax.random.randint(jax.random.fold_in(key, 13), (), 0, TOKENS - 1)) % TOKENS
    return drawn.at[shortest].set(2).at[longest].set(CACHE_LEN).astype(jnp.int32)


def draw_live_counts(key, part):
    devices_total = TOKENS // TOKENS_PER_UNIT
    smallest_value = 3 * TOKENS_PER_UNIT // 4
    drawn = jax.random.randint(jax.random.fold_in(key, 21), (devices_total,), smallest_value, TOKENS_PER_UNIT + 1)
    fullest = jax.random.randint(jax.random.fold_in(key, 22), (), 0, devices_total)
    emptiest = (fullest + 1 + jax.random.randint(jax.random.fold_in(key, 23), (), 0, devices_total - 1)) % devices_total
    return drawn.at[emptiest].set(smallest_value).at[fullest].set(TOKENS_PER_UNIT).astype(jnp.int32)


def level_of(rng, extent, cuts, smallest, largest):
    level, own = 1.0, jax.random.fold_in(rng, 6)
    for dim, blocks in cuts:
        heights = jnp.exp(jax.random.uniform(jax.random.fold_in(own, dim), (blocks,), jnp.float32, smallest / len(cuts), largest / len(cuts)))
        level = level * jnp.repeat(heights, extent[dim] // blocks).reshape([-1 if axis == dim else 1 for axis in range(len(extent))])
    return level


def assign_block(stream_key, own, number, rows, amount, top, limit, slope):
    sequence = jax.random.permutation(stream_key, amount)
    heavy_load, ordinary = load_shares(amount, rows * top, limit, slope, True), load_shares(amount, rows * top, limit, slope, False)
    places = jnp.arange(amount)

    def named(sizes, offset_by):
        used = int((sizes > 0).sum())
        fixed = max(1, used // 4)
        shifted = fixed + (places - fixed + offset_by * (used - fixed)) % max(1, amount - fixed)
        return jnp.zeros((amount,), jnp.int32).at[sequence[jnp.where(places < fixed, places, shifted)]].set(jnp.asarray(sizes, jnp.int32))

    sizes = jnp.where(number % 4 == 0, named(heavy_load, number // 4), named(ordinary, number - number // 4 - 1))
    mixed = jax.random.permutation(jax.random.fold_in(own, 3), amount)
    giver, sink = mixed[0:amount // 2 * 2:2], mixed[1:amount // 2 * 2:2]
    slack = jnp.minimum(sizes[giver] - 1, limit - sizes[sink]) // 2
    slack = jnp.where((giver == sequence[0]) | (sink == sequence[0]) | (sizes[sink] == 0), 0, jnp.maximum(slack, 0))
    shifted = jax.random.randint(jax.random.fold_in(own, 4), (amount // 2,), 0, 1 << 20) % (slack + 1)
    sizes = sizes.at[giver].add(-shifted).at[sink].add(shifted)
    items = jnp.searchsorted(jnp.cumsum(sizes), jnp.arange(rows * top), side="right").astype(jnp.int32)
    table = items.reshape(top, rows).T
    table = table[jax.random.permutation(jax.random.fold_in(own, 1), rows)]
    offset_by = jax.random.randint(jax.random.fold_in(own, 2), (rows, 1), 0, top)
    return jnp.take_along_axis(table, (jnp.arange(top)[None, :] + offset_by) % top, axis=1)


def load_shares(amount, total, most, skew, full):
    portions = [(1 << 20) // math.isqrt(grade ** skew) + 1 for grade in range(1, amount + 1)]
    largest = most if full else min(most, max(-(-total // amount), total * portions[0] // sum(portions)))
    least = 1 if total - largest >= amount - 1 else 0
    holding, surplus = [largest] + [least] * (amount - 1), total - largest - least * (amount - 1)
    while surplus > 0:
        candidates = [i for i in range(1, amount) if holding[i] < largest] or [i for i in range(1, amount) if holding[i] < most]
        whole, left = sum([portions[i] for i in candidates]), surplus
        for i in candidates:
            more = min(most - holding[i], max(1, left * portions[i] // whole), surplus)
            holding[i] = holding[i] + more
            surplus = surplus - more
    return np.array(holding)


def gaussian(key, dims, width, bound, shards=(), kind=jnp.bfloat16):
    values = jax.random.normal(key, dims, jnp.float32) * width
    if len(shards) > 0:
        values = level_of(key, dims, shards, -0.22, 0.18) * values
    return jnp.clip(values, min=-bound, max=bound).astype(kind)


def setup_inputs(seed: int = 0) -> dict:
    key_list = jax.random.split(jax.random.key(seed), 13)
    hidden_in = gaussian(key_list[0], (TOKENS, D), 1.0, 6.0, ((0, 32),))
    queries = draw_queries(jax.random.fold_in(key_list[12], 71), 0)
    latent_cache = draw_latent_cache(jax.random.fold_in(key_list[12], 71), 0)
    lengths = draw_lengths(jax.random.fold_in(key_list[12], 71), 0)
    w_uv = gaussian(key_list[4], (HEAD_BLOCK, HEADS // HEAD_BLOCK, KV_RANK, V_DIM), (KV_RANK // 8) ** -0.5, 0.75)
    attn_weight = gaussian(key_list[5], (HEAD_BLOCK, HEADS // HEAD_BLOCK, V_DIM, D), (HEAD_BLOCK * V_DIM) ** -0.5, 0.046875, ((3, 16),))
    norm_gain = jnp.clip(1.0 + 0.18 * jax.random.normal(key_list[6], (D,), jnp.float32), 0.1, 1.9)
    router = gaussian(key_list[7], (D, EXPERTS), D ** -0.5, 0.0625)
    routes_keys = jax.random.split(jax.random.fold_in(key_list[8], 1), TOKENS // TOKENS_PER_UNIT)
    routes_turns = jax.random.permutation(jax.random.fold_in(key_list[8], 3), TOKENS // TOKENS_PER_UNIT)
    routes = jax.vmap(lambda own, number: assign_block(jax.random.fold_in(key_list[8], 2), own, number, TOKENS_PER_UNIT, EXPERTS, TOPK, MOST, 2))(routes_keys, routes_turns).reshape((TOKENS, TOPK))
    live_counts = draw_live_counts(jax.random.fold_in(key_list[12], 71), 0)
    expert_in = gaussian(key_list[10], (EXPERTS, D, 2, HID), D ** -0.5, 0.0625, ((0, 32),))
    expert_out = gaussian(key_list[11], (EXPERTS, HID, D), (HID // 8) ** -0.5, 0.5, ((0, 32),))
    return dict(hidden_in=hidden_in, queries=queries, latent_cache=latent_cache, lengths=lengths, w_uv=w_uv, attn_weight=attn_weight, norm_gain=norm_gain, router=router, routes=routes, live_counts=live_counts, expert_in=expert_in, expert_out=expert_out)


score_scale = 192.0 ** (-0.5)
route_scale = 2.5

def routed_experts(normalized_input, routes, gate_weights, expert_in, expert_out):
    pair_total = TOKENS * TOPK
    pair_expert = routes.reshape(pair_total).astype(jnp.int32)
    pair_token = (jnp.arange(pair_total) // TOPK).astype(jnp.int32)
    pair_gate = gate_weights.reshape(pair_total)
    ordering = jnp.argsort(pair_expert, stable=True)
    sorted_token = pair_token[ordering]
    sorted_gate = pair_gate[ordering]
    expert_ids = jnp.arange(EXPERTS).astype(jnp.int32)
    starts = lax.optimization_barrier(jnp.sum((pair_expert[None, :] < expert_ids[:, None]).astype(jnp.int32), axis=1))
    finishes = starts + lax.optimization_barrier(jnp.sum((pair_expert[None, :] == expert_ids[:, None]).astype(jnp.int32), axis=1))
    window = TOKENS // TOKENS_PER_UNIT * MOST
    offsets = jnp.arange(window).astype(jnp.int32)
    slice_width = HID // N_TP

    def one_expert(total, inputs):
        weight_in, weight_out, start, finish = inputs
        position = start + offsets
        inside = position < finish
        clipped = jnp.minimum(position, pair_total - 1)
        token_matrix_rows = sorted_token[clipped]
        gathered = normalized_input[token_matrix_rows]
        gate_up = jnp.dot(gathered, weight_in.reshape(D, 2 * HID), preferred_element_type=jnp.float32)
        activated = (jax.nn.silu(gate_up[:, :HID]) * gate_up[:, HID:]).astype(jnp.bfloat16)
        pieces = jnp.einsum('wsk,skd->wsd', activated.reshape(window, N_TP, slice_width).astype(jnp.float32), weight_out.reshape(N_TP, slice_width, D).astype(jnp.float32)).astype(jnp.bfloat16)
        expert_value = lax.optimization_barrier(jnp.sum(pieces.astype(jnp.float32), axis=1))
        factor = jnp.where(inside, sorted_gate[clipped], jnp.zeros_like(sorted_gate[clipped]))
        return (total.at[token_matrix_rows].add(expert_value * factor[:, None]), None)
    total, _ = lax.scan(one_expert, jnp.zeros((TOKENS, D), jnp.float32), (expert_in, expert_out, starts, finishes))
    return total

def reference(hidden_in, queries, latent_cache, lengths, w_uv, attn_weight, norm_gain, router, routes, live_counts, expert_in, expert_out):
    query_all = queries.reshape(TOKENS, HEADS, QK_DIM).astype(jnp.float32)
    cache_all = latent_cache.astype(jnp.float32)
    scores = jnp.einsum('jhr,jpr->jhp', query_all, cache_all) * score_scale
    positions = jnp.arange(CACHE_LEN).astype(jnp.int32)
    visible = positions[None, None, :] < lengths[:, None, None]
    scores = jnp.where(visible, scores, jnp.full_like(scores, -1e+30))
    highest = lax.optimization_barrier(jnp.max(scores, axis=2, keepdims=True))
    raised = jnp.exp(scores - highest)
    softmax_weights = (raised / lax.optimization_barrier(jnp.sum(raised, axis=2, keepdims=True))).astype(jnp.bfloat16)
    latent_out = jnp.einsum('jhp,jpc->jhc', softmax_weights.astype(jnp.float32), cache_all[:, :, :KV_RANK]).astype(jnp.bfloat16)
    up_proj = w_uv.reshape(HEADS, KV_RANK, V_DIM).astype(jnp.float32)
    head_out = jnp.einsum('jhc,hcv->jhv', latent_out.astype(jnp.float32), up_proj).astype(jnp.bfloat16)
    attention = jnp.dot(head_out.reshape(TOKENS, HEADS * V_DIM), attn_weight.reshape(HEADS * V_DIM, D), preferred_element_type=jnp.float32).astype(jnp.bfloat16)
    residual = hidden_in.astype(jnp.float32) + attention.astype(jnp.float32)
    normalized_input = (residual * lax.rsqrt(lax.optimization_barrier(jnp.mean(residual * residual, axis=1, keepdims=True)) + 1e-06) * norm_gain).astype(jnp.bfloat16)
    affinity = jax.nn.sigmoid(jnp.dot(normalized_input, router, preferred_element_type=jnp.float32))
    chosen = jnp.take_along_axis(affinity, routes, axis=1)
    token_ids = jnp.arange(TOKENS).astype(jnp.int32)
    living = (token_ids % TOKENS_PER_UNIT < live_counts[token_ids // TOKENS_PER_UNIT]).astype(jnp.float32)
    gate_weights = route_scale * chosen / lax.optimization_barrier(jnp.sum(chosen, axis=1, keepdims=True)) * living[:, None]
    expert_mix = routed_experts(normalized_input, routes, gate_weights, expert_in, expert_out)
    return (residual + expert_mix).astype(jnp.bfloat16)
```

```python
import functools

import jax
import jax.numpy as jnp
from jax import lax
from jax.experimental import pallas as pl
from jax.experimental.pallas import tpu as pltpu
from jax.sharding import PartitionSpec as P

score_scale = 192.0 ** (-0.5)
route_scale = 2.5


def divisor_at_most(number, most):
    return max(d for d in range(1, most + 1) if number % d == 0)


def project_kernel(heads_step, x_ref, w_ref, out_ref, total):
    step = pl.program_id(0)

    @pl.when(step == 0)
    def _():
        total[...] = jnp.zeros_like(total)

    value_width = w_ref.shape[2]
    part = jnp.zeros(total.shape, jnp.float32)
    pair = 2 if heads_step % 2 == 0 else 1
    for i in range(0, heads_step, pair):
        block = jnp.concatenate([w_ref[i + k] for k in range(pair)], axis=1)
        part += lax.dot_general(
            x_ref[:, i * value_width : (i + pair) * value_width],
            block,
            (((1,), (1,)), ((), ())),
            preferred_element_type=jnp.float32,
        )
    total[...] += part

    @pl.when(step == pl.num_programs(0) - 1)
    def _():
        out_ref[...] = total[...].astype(out_ref.dtype)


def project(rows, weight):
    heads, columns, value_width = weight.shape
    tokens = rows.shape[0]
    heads_step = divisor_at_most(heads, 8)
    return pl.pallas_call(
        functools.partial(project_kernel, heads_step),
        grid=(heads // heads_step,),
        in_specs=[
            pl.BlockSpec((tokens, heads_step * value_width), lambda i: (0, i)),
            pl.BlockSpec((heads_step, columns, value_width), lambda i: (i, 0, 0)),
        ],
        out_specs=pl.BlockSpec((tokens, columns), lambda i: (0, 0)),
        out_shape=jax.ShapeDtypeStruct((tokens, columns), jnp.float32),
        scratch_shapes=[pltpu.VMEM((tokens, columns), jnp.float32)],
        compiler_params=pltpu.CompilerParams(vmem_limit_bytes=16 * 1024 * 1024),
        cost_estimate=pl.CostEstimate(
            flops=2 * tokens * heads * value_width * columns,
            bytes_accessed=2 * heads * value_width * (columns + tokens),
            transcendentals=0,
        ),
        name="project",
    )(rows, weight)


def shards(
    hidden_in,
    queries,
    latent_cache,
    lengths,
    w_uv,
    attn_weight,
    norm_gain,
    router,
    routes,
    live_counts,
    expert_in,
    expert_out,
):
    everyone = ("sec", "grp", "tp")
    own_tokens, width = hidden_in.shape
    sections = lax.axis_size("sec")
    expert_groups = lax.axis_size("grp")
    latent_width = w_uv.shape[2]
    experts = router.shape[1]

    picked = jnp.any(routes[:, :, None] == jnp.arange(experts)[None, None, :], axis=1)
    living = jnp.arange(own_tokens) < live_counts[0]
    chosen_mask = (picked & living[:, None]).astype(jnp.float32)
    mask_all = lax.all_gather(chosen_mask, everyone, axis=0, tiled=True)
    hidden_all = lax.all_gather(hidden_in, everyone, axis=0, tiled=True)

    query_block = queries[:, :, 0, :]
    scores = (
        jnp.einsum("bhr,bpr->bhp", query_block, latent_cache, preferred_element_type=jnp.float32)
        * score_scale
    )
    positions = jnp.arange(latent_cache.shape[1])
    visible = positions[None, None, :] < lengths[:, None, None]
    scores = jnp.where(visible, scores, -1e30)
    highest = jnp.max(scores, axis=2, keepdims=True)
    raised = jnp.exp(scores - highest)
    softmax_weights = (raised / jnp.sum(raised, axis=2, keepdims=True)).astype(jnp.bfloat16)
    latent_out = jnp.einsum(
        "bhp,bpc->bhc",
        softmax_weights,
        latent_cache[:, :, :latent_width],
        preferred_element_type=jnp.float32,
    ).astype(jnp.bfloat16)
    head_out = jnp.einsum(
        "bhc,hcv->bhv", latent_out, w_uv[:, 0], preferred_element_type=jnp.float32
    ).astype(jnp.bfloat16)
    head_rows = head_out.reshape(head_out.shape[0], -1)
    group_rows = lax.all_gather(head_rows, "grp", axis=0, tiled=True)
    column_part = project(group_rows, jnp.transpose(attn_weight[:, 0], (0, 2, 1)))
    if lax.axis_size("tp") > 1:
        column_part = lax.psum(column_part, "tp")
    column_part = column_part.astype(jnp.bfloat16)
    gathered = lax.all_gather(column_part, ("sec", "grp"), axis=0, tiled=False)
    section_tokens, columns = column_part.shape
    attention = (
        gathered.reshape(sections, expert_groups, section_tokens, columns)
        .transpose(0, 2, 1, 3)
        .reshape(sections * section_tokens, width)
    )
    residual = hidden_all.astype(jnp.float32) + attention.astype(jnp.float32)
    normed = (
        residual
        * lax.rsqrt(jnp.mean(residual * residual, axis=1, keepdims=True) + 1e-06)
        * norm_gain
    ).astype(jnp.bfloat16)
    affinity = jax.nn.sigmoid(jnp.dot(normed, router, preferred_element_type=jnp.float32))
    chosen = affinity * mask_all
    live_all = jnp.max(mask_all, axis=1, keepdims=True) > 0.0
    gate_all = jnp.where(
        live_all, route_scale * chosen / jnp.sum(chosen, axis=1, keepdims=True), 0.0
    )
    group = lax.axis_index("sec") * expert_groups + lax.axis_index("grp")
    own_gate = jnp.sum(
        jnp.where(jnp.arange(experts)[None, :] == group, gate_all, 0.0), axis=1, keepdims=True
    )

    slice_width = expert_in.shape[3]
    gate_up = jnp.dot(
        normed, expert_in[0].reshape(width, 2 * slice_width), preferred_element_type=jnp.float32
    )
    activated = (jax.nn.silu(gate_up[:, :slice_width]) * gate_up[:, slice_width:]).astype(
        jnp.bfloat16
    )
    value = jnp.dot(activated, expert_out[0], preferred_element_type=jnp.float32)
    mixed = (value * own_gate).astype(jnp.bfloat16)
    expert_mix = lax.psum_scatter(mixed, everyone, scatter_dimension=0, tiled=True)
    place = group * lax.axis_size("tp") + lax.axis_index("tp")
    own_attention = lax.dynamic_slice_in_dim(attention, place * own_tokens, own_tokens, 0)
    own_residual = hidden_in.astype(jnp.float32) + own_attention.astype(jnp.float32)
    return (own_residual + expert_mix.astype(jnp.float32)).astype(jnp.bfloat16)


def solution(mesh):
    placed = (
        P(("sec", "grp", "tp"), None),
        P(("sec", "grp"), None, "tp", None),
        P(("sec", "grp"), None, None),
        P(("sec", "grp")),
        P(None, "tp", None, None),
        P(None, "tp", None, "grp"),
        P(),
        P(),
        P(("sec", "grp", "tp"), None),
        P(("sec", "grp", "tp")),
        P(("sec", "grp"), None, None, "tp"),
        P(("sec", "grp"), "tp", None),
    )
    return jax.shard_map(
        shards, mesh=mesh, in_specs=placed, out_specs=P(("sec", "grp", "tp"), None), check_vma=False
    )
```

```python
import functools

import jax
import jax.numpy as jnp
from jax import lax
from jax.experimental import pallas as pl
from jax.experimental.pallas import tpu as pltpu
from jax.sharding import PartitionSpec as P

score_scale = 192.0 ** (-0.5)
route_scale = 2.5


def divisor_at_most(number, most):
    return max(d for d in range(1, most + 1) if number % d == 0)


def project_kernel(heads_step, x_ref, w_ref, out_ref, total):
    step = pl.program_id(0)

    @pl.when(step == 0)
    def _():
        total[...] = jnp.zeros_like(total)

    value_width = w_ref.shape[2]
    part = jnp.zeros(total.shape, jnp.float32)
    pair = 2 if heads_step % 2 == 0 else 1
    for i in range(0, heads_step, pair):
        block = jnp.concatenate([w_ref[i + k] for k in range(pair)], axis=1)
        part += lax.dot_general(
            x_ref[:, i * value_width : (i + pair) * value_width],
            block,
            (((1,), (1,)), ((), ())),
            preferred_element_type=jnp.float32,
        )
    total[...] += part

    @pl.when(step == pl.num_programs(0) - 1)
    def _():
        out_ref[...] = total[...].astype(out_ref.dtype)


def project(rows, weight):
    heads, columns, value_width = weight.shape
    tokens = rows.shape[0]
    heads_step = divisor_at_most(heads, 8)
    return pl.pallas_call(
        functools.partial(project_kernel, heads_step),
        grid=(heads // heads_step,),
        in_specs=[
            pl.BlockSpec((tokens, heads_step * value_width), lambda i: (0, i)),
            pl.BlockSpec((heads_step, columns, value_width), lambda i: (i, 0, 0)),
        ],
        out_specs=pl.BlockSpec((tokens, columns), lambda i: (0, 0)),
        out_shape=jax.ShapeDtypeStruct((tokens, columns), jnp.float32),
        scratch_shapes=[pltpu.VMEM((tokens, columns), jnp.float32)],
        compiler_params=pltpu.CompilerParams(vmem_limit_bytes=16 * 1024 * 1024),
        cost_estimate=pl.CostEstimate(
            flops=2 * tokens * heads * value_width * columns,
            bytes_accessed=2 * heads * value_width * (columns + tokens),
            transcendentals=0,
        ),
        name="project",
    )(rows, weight)

MESH = pl.DeviceIdType.MESH


def flip(index, bit):
    return index + bit - 2 * bit * lax.rem(index // bit, 2)


def partner(bit):
    axis, value = bit
    return {axis: flip(lax.axis_index(axis), value)}


def greet(bits):
    barrier = pltpu.get_barrier_semaphore()
    for bit in bits:
        pl.semaphore_signal(barrier, inc=1, device_id=partner(bit), device_id_type=MESH)
    pl.semaphore_wait(barrier, len(bits))


def axis_bits(axis, size):
    return [(axis, 1 << k) for k in reversed(range(size.bit_length() - 1))]


def gather_kernel(orders, spans, flat, x_ref, out_ref, send_sems, recv_sems, own_sem):
    bits = orders[0]
    greet(bits)

    def block(subset, order):
        place = {axis: lax.axis_index(axis) for axis in flat}
        for k, (axis, value) in enumerate(order):
            if subset >> k & 1:
                place[axis] = flip(place[axis], value)
        index = 0
        for axis, size in flat.items():
            index = index * size + place[axis]
        return index

    def move(chunk, order, step, subset):
        first, count = spans[chunk]
        slot = out_ref.at[block(subset, order), pl.ds(first, count)]
        source = x_ref.at[pl.ds(first, count)] if subset == 0 else slot
        which = (1 << step) - 1 + subset
        return pltpu.make_async_remote_copy(
            src_ref=source,
            dst_ref=slot,
            send_sem=send_sems.at[chunk, which],
            recv_sem=recv_sems.at[chunk, which],
            device_id=partner(order[step]),
            device_id_type=MESH,
        )

    for step in range(len(bits)):
        for chunk, order in enumerate(orders):
            move(chunk, order, step, 0).start()
    own = pltpu.make_async_copy(x_ref, out_ref.at[block(0, bits)], own_sem)
    own.start()
    for step in range(len(bits)):
        for subset in range(1 << step):
            for chunk, order in enumerate(orders):
                move(chunk, order, step, subset).wait_recv()
                for later in range(step + 1, len(bits)):
                    move(chunk, order, later, subset + (1 << step)).start()
    for step in range(len(bits)):
        for subset in range(1 << step):
            for chunk, order in enumerate(orders):
                move(chunk, order, step, subset).wait_send()
    own.wait()


def gather(block, orders, flat, collective_id, name):
    rows, columns = block.shape
    blocks = 1
    for size in flat.values():
        blocks *= size
    count = rows // len(orders)
    spans = [(k * count, count) for k in range(len(orders))]
    return pl.pallas_call(
        functools.partial(gather_kernel, orders, spans, flat),
        out_shape=jax.ShapeDtypeStruct((blocks, rows, columns), block.dtype),
        in_specs=[pl.BlockSpec(memory_space=pltpu.VMEM)],
        out_specs=pl.BlockSpec(memory_space=pltpu.VMEM),
        scratch_shapes=[
            pltpu.SemaphoreType.DMA((len(orders), blocks - 1)),
            pltpu.SemaphoreType.DMA((len(orders), blocks - 1)),
            pltpu.SemaphoreType.DMA,
        ],
        compiler_params=pltpu.CompilerParams(
            collective_id=collective_id, has_side_effects=True, vmem_limit_bytes=40 * 1024 * 1024
        ),
        name=name,
    )(block)


def reduce_kernel(core, halving, whole_bits, orders, x_ref, out_ref, summed, from_core, half_in,
                  whole_in, core_sems, half_sems, whole_sems, end_sems):
    greet([core] + halving + whole_bits)
    groups, rows, width = x_ref.shape
    half = width // 2
    part = half // len(orders)
    side = lax.rem(lax.axis_index(core[0]) // core[1], 2)
    mine = pl.ds(pl.multiple_of(side * half, 128), half)
    other = pl.ds(pl.multiple_of((1 - side) * half, 128), half)
    my_bit = {bit: lax.rem(lax.axis_index(bit[0]) // bit[1], 2) for bit in halving}

    def group_of(done, current, sent, rest):
        index, place = 0, 0
        for bit in halving:
            if bit in done:
                value = my_bit[bit]
            elif bit == current:
                value = (1 - my_bit[bit]) if sent else my_bit[bit]
            else:
                value = rest >> place & 1
                place += 1
            index = index * 2 + value
        return index

    def remote(source, target, sems, device):
        return pltpu.make_async_remote_copy(
            src_ref=source, dst_ref=target, send_sem=sems.at[0], recv_sem=sems.at[1],
            device_id=partner(device), device_id_type=MESH,
        )

    def add(first, second):
        return (first.astype(jnp.float32) + second.astype(jnp.float32)).astype(jnp.bfloat16)

    pending = []
    firsts = [
        remote(x_ref.at[g, :, other], from_core.at[g], core_sems.at[g], core)
        for g in range(groups)
    ]
    for copy in firsts:
        copy.start()
    for g in range(groups):
        firsts[g].wait_recv()
        summed[g] = add(x_ref[g, :, mine], from_core[g])
    pending += firsts
    steps = len(halving)
    slots = [0]
    for step in range(steps):
        slots.append(slots[-1] + (1 << (steps - 1 - step)))

    def halve(step, chunk, rest):
        order = orders[chunk]
        span = pl.ds(chunk * part, part)
        slot = slots[step] + rest
        return remote(
            summed.at[group_of(order[:step], order[step], True, rest), :, span],
            half_in.at[slot, :, span],
            half_sems.at[chunk, slot],
            order[step],
        )

    for step in range(steps):
        for chunk in range(len(orders)):
            for rest in range(1 << (steps - 1 - step)):
                copy = halve(step, chunk, rest)
                copy.start()
                pending.append(copy)
        for chunk, order in enumerate(orders):
            span = pl.ds(chunk * part, part)
            for rest in range(1 << (steps - 1 - step)):
                halve(step, chunk, rest).wait_recv()
                g = group_of(order[:step], order[step], False, rest)
                summed[g, :, span] = add(
                    summed[g, :, span], half_in[slots[step] + rest, :, span]
                )
    group = group_of(halving, None, False, 0)
    current = summed[group]
    for k, bit in enumerate(whole_bits):
        whole_in[k, 0] = current
        copy = remote(whole_in.at[k, 0], whole_in.at[k, 1], whole_sems.at[k], bit)
        copy.start()
        copy.wait_recv()
        pending.append(copy)
        current = add(whole_in[k, 0], whole_in[k, 1])
    out_ref[:, mine] = current
    last = remote(out_ref.at[:, mine], out_ref.at[:, mine], end_sems, core)
    last.start()
    last.wait_recv()
    pending.append(last)
    for copy in pending:
        copy.wait_send()


def reduce_rows(values, core, halving, whole_bits, orders, collective_id):
    groups, rows, width = values.shape
    half = width // 2
    dma = pltpu.SemaphoreType.DMA
    return pl.pallas_call(
        functools.partial(reduce_kernel, core, halving, whole_bits, orders),
        out_shape=jax.ShapeDtypeStruct((rows, width), values.dtype),
        in_specs=[pl.BlockSpec(memory_space=pltpu.VMEM)],
        out_specs=pl.BlockSpec(memory_space=pltpu.VMEM),
        scratch_shapes=[
            pltpu.VMEM((groups, rows, half), jnp.bfloat16),
            pltpu.VMEM((groups, rows, half), jnp.bfloat16),
            pltpu.VMEM((groups - 1, rows, half), jnp.bfloat16),
            pltpu.VMEM((len(whole_bits), 2, rows, half), jnp.bfloat16),
            dma((groups, 2)),
            dma((len(orders), groups - 1, 2)),
            dma((len(whole_bits), 2)),
            dma((2,)),
        ],
        compiler_params=pltpu.CompilerParams(
            collective_id=collective_id, has_side_effects=True, vmem_limit_bytes=56 * 1024 * 1024
        ),
        name="reduce_rows",
    )(values)


def shards(
    hidden_in,
    queries,
    latent_cache,
    lengths,
    w_uv,
    attn_weight,
    norm_gain,
    router,
    routes,
    live_counts,
    expert_in,
    expert_out,
):
    own_tokens, width = hidden_in.shape
    sections = lax.axis_size("sec")
    expert_groups = lax.axis_size("grp")
    latent_width = w_uv.shape[2]
    experts = router.shape[1]

    tp = lax.axis_size("tp")
    grp_bits = axis_bits("grp", expert_groups)
    sec_bits = axis_bits("sec", sections)
    core, low, rest_bits = grp_bits[-1], grp_bits[-2], grp_bits[:-2]
    flat = {"sec": sections, "grp": expert_groups}

    picked = jnp.any(routes[:, :, None] == jnp.arange(experts)[None, None, :], axis=1)
    living = jnp.arange(own_tokens) < live_counts[0]
    unit_mask = (picked & living[:, None]).astype(jnp.bfloat16)
    unit_hidden = hidden_in
    if tp > 1:
        unit_mask = lax.all_gather(unit_mask, "tp", axis=0, tiled=True)
        unit_hidden = lax.all_gather(unit_hidden, "tp", axis=0, tiled=True)
    unit = unit_hidden.shape[0]
    hidden_part = lax.all_to_all(unit_hidden, "grp", split_axis=1, concat_axis=0, tiled=True)

    query_block = queries[:, :, 0, :]
    scores = (
        jnp.einsum("bhr,bpr->bhp", query_block, latent_cache, preferred_element_type=jnp.float32)
        * score_scale
    )
    positions = jnp.arange(latent_cache.shape[1])
    visible = positions[None, None, :] < lengths[:, None, None]
    scores = jnp.where(visible, scores, -1e30)
    highest = jnp.max(scores, axis=2, keepdims=True)
    raised = jnp.exp(scores - highest)
    softmax_weights = (raised / jnp.sum(raised, axis=2, keepdims=True)).astype(jnp.bfloat16)
    latent_out = jnp.einsum(
        "bhp,bpc->bhc",
        softmax_weights,
        latent_cache[:, :, :latent_width],
        preferred_element_type=jnp.float32,
    ).astype(jnp.bfloat16)
    head_out = jnp.einsum(
        "bhc,hcv->bhv", latent_out, w_uv[:, 0], preferred_element_type=jnp.float32
    ).astype(jnp.bfloat16)
    parts = max(1, 32 // unit)
    head_rows = head_out.reshape(unit, parts, -1).transpose(1, 0, 2).reshape(parts * unit, -1)
    group_blocks = gather(
        head_rows,
        [rest_bits + [low, core], rest_bits + [low, core]],
        {"grp": expert_groups},
        0,
        "gather_heads",
    )
    group_rows = (
        group_blocks.reshape(expert_groups, parts, unit, -1)
        .transpose(0, 2, 1, 3)
        .reshape(expert_groups * unit, -1)
    )
    column_part = project(group_rows, jnp.transpose(attn_weight[:, 0], (0, 2, 1)))
    if lax.axis_size("tp") > 1:
        column_part = lax.psum(column_part, "tp")
    column_part = column_part.astype(jnp.bfloat16).astype(jnp.float32)
    residual_part = (column_part + hidden_part.astype(jnp.float32)).astype(jnp.bfloat16)
    section_tokens, columns = residual_part.shape
    mask_block = jnp.pad(unit_mask, ((0, section_tokens - unit), (0, 0)))
    gathered = gather(
        jnp.concatenate([residual_part, mask_block], axis=1),
        [rest_bits + [low] + sec_bits + [core], sec_bits + [low] + rest_bits + [core]],
        flat,
        1,
        "gather_columns",
    )
    depth = len(grp_bits) - 1

    def reorder(rows):
        split = rows.reshape([sections] + [2] * depth + [2 * unit, rows.shape[-1]])
        turned = split.transpose([0] + list(range(depth, 0, -1)) + [depth + 1, depth + 2])
        return turned.reshape(-1, rows.shape[-1])

    mask_all = reorder(gathered[:, :unit, columns:].reshape(-1, experts)).astype(jnp.float32)
    residual = (
        gathered[:, :, :columns]
        .reshape([sections, expert_groups] + [2] * depth + [2 * unit, columns])
        .transpose([0] + list(range(depth + 1, 1, -1)) + [depth + 2, 1, depth + 3])
        .reshape(sections * section_tokens, width)
        .astype(jnp.float32)
    )
    normed = (
        residual
        * lax.rsqrt(jnp.mean(residual * residual, axis=1, keepdims=True) + 1e-06)
        * norm_gain
    ).astype(jnp.bfloat16)
    affinity = jax.nn.sigmoid(jnp.dot(normed, router, preferred_element_type=jnp.float32))
    chosen = affinity * mask_all
    live_all = jnp.max(mask_all, axis=1, keepdims=True) > 0.0
    gate_all = jnp.where(
        live_all, route_scale * chosen / jnp.sum(chosen, axis=1, keepdims=True), 0.0
    )
    group = lax.axis_index("sec") * expert_groups + lax.axis_index("grp")
    own_gate = jnp.sum(
        jnp.where(jnp.arange(experts)[None, :] == group, gate_all, 0.0), axis=1, keepdims=True
    )

    slice_width = expert_in.shape[3]
    gate_up = jnp.dot(
        normed, expert_in[0].reshape(width, 2 * slice_width), preferred_element_type=jnp.float32
    )
    activated = (jax.nn.silu(gate_up[:, :slice_width]) * gate_up[:, slice_width:]).astype(
        jnp.bfloat16
    )
    value = jnp.dot(activated, expert_out[0], preferred_element_type=jnp.float32)
    mixed = (value * own_gate).astype(jnp.bfloat16)
    grain = 4 * unit
    halving = sec_bits + [low] + list(reversed(rest_bits))[:-1]
    swapped = [low] + sec_bits + list(reversed(rest_bits))[:-1]
    mixed = mixed.reshape(-1, grain, width)
    shared = reduce_rows(mixed, core, halving, rest_bits[:1], [halving, swapped], 2)
    place = lax.axis_index("grp")
    quarter = (place // rest_bits[0][1]) % 2 * 2 + place % 2
    if tp > 1:
        owned = lax.dynamic_slice_in_dim(shared, quarter * unit, unit, 0)
        expert_mix = lax.psum_scatter(owned, "tp", scatter_dimension=0, tiled=True)
    else:
        expert_mix = lax.dynamic_slice_in_dim(shared, quarter * unit, unit, 0)
    own_row = 0
    for axis, value in halving + rest_bits[:1]:
        own_row = own_row * 2 + (lax.axis_index(axis) // value) % 2
    own_row = (own_row * 2 + place % 2) * unit + lax.axis_index("tp") * own_tokens
    own_residual = lax.dynamic_slice_in_dim(residual, own_row, own_tokens, 0)
    return (own_residual + expert_mix.astype(jnp.float32)).astype(jnp.bfloat16)


def expert_slice(rows_in, expert_in, expert_out):
    width = rows_in.shape[1]
    slice_width = expert_in.shape[3]
    gate_up = jnp.dot(
        rows_in, expert_in[0].reshape(width, 2 * slice_width), preferred_element_type=jnp.float32
    )
    activated = (jax.nn.silu(gate_up[:, :slice_width]) * gate_up[:, slice_width:]).astype(
        jnp.bfloat16
    )
    return jnp.dot(activated, expert_out[0], preferred_element_type=jnp.float32).astype(
        jnp.bfloat16
    )


def shards_split(
    hidden_in,
    queries,
    latent_cache,
    lengths,
    w_uv,
    attn_weight,
    norm_gain,
    router,
    routes,
    live_counts,
    expert_in,
    expert_out,
):
    count_of_tokens, width = hidden_in.shape
    sections = lax.axis_size("sec")
    expert_groups = lax.axis_size("grp")
    slices = lax.axis_size("tp")
    latent_width = w_uv.shape[2]
    query_block = queries[:, :, 0, :]
    scores = (
        jnp.einsum("bhr,bpr->bhp", query_block, latent_cache, preferred_element_type=jnp.float32)
        * score_scale
    )
    positions = jnp.arange(latent_cache.shape[1])
    visible = positions[None, None, :] < lengths[:, None, None]
    scores = jnp.where(visible, scores, -1e30)
    highest = jnp.max(scores, axis=2, keepdims=True)
    raised = jnp.exp(scores - highest)
    softmax_weights = (raised / jnp.sum(raised, axis=2, keepdims=True)).astype(jnp.bfloat16)
    latent_out = jnp.einsum(
        "bhp,bpc->bhc",
        softmax_weights,
        latent_cache[:, :, :latent_width],
        preferred_element_type=jnp.float32,
    ).astype(jnp.bfloat16)
    head_out = jnp.einsum(
        "bhc,hcv->bhv", latent_out, w_uv[:, 0], preferred_element_type=jnp.float32
    ).astype(jnp.bfloat16)
    head_rows = head_out.reshape(head_out.shape[0], -1)
    out_block = attn_weight[:, 0].reshape(-1, attn_weight.shape[3])
    partial_value = jnp.dot(
        lax.all_gather(head_rows, "grp", axis=0, tiled=True),
        out_block,
        preferred_element_type=jnp.float32,
    )
    partial_value = partial_value.reshape(
        expert_groups, slices, count_of_tokens, partial_value.shape[1]
    )
    summed = lax.psum_scatter(
        partial_value.astype(jnp.bfloat16), "tp", scatter_dimension=1, tiled=True
    ).astype(jnp.float32)
    column_part = summed[:, 0].astype(jnp.bfloat16)
    attention = lax.all_to_all(column_part, "grp", split_axis=0, concat_axis=2, tiled=True)[0]
    residual = hidden_in.astype(jnp.float32) + attention.astype(jnp.float32)
    normalized_input = (
        residual
        * lax.rsqrt(jnp.mean(residual * residual, axis=1, keepdims=True) + 1e-06)
        * norm_gain
    ).astype(jnp.bfloat16)
    experts = router.shape[1]
    per_token = routes.shape[1]
    capacity = max(2, 2 * count_of_tokens * per_token // experts)
    affinity = jax.nn.sigmoid(jnp.dot(normalized_input, router, preferred_element_type=jnp.float32))
    picked = routes[:, :, None] == jnp.arange(experts)[None, None, :]
    chosen = jnp.sum(jnp.where(picked, affinity[:, None, :], 0.0), axis=2)
    living = jnp.arange(count_of_tokens) < live_counts[0]
    gate_weights = (
        route_scale
        * chosen
        / jnp.sum(chosen, axis=1, keepdims=True)
        * living[:, None].astype(jnp.float32)
    )
    routed = jnp.any(picked, axis=1) & living[:, None]
    routed_count = routed.astype(jnp.int32)
    slot_index = jnp.cumsum(routed_count, axis=0) - routed_count
    placed_tokens = routed[:, :, None] & (
        slot_index[:, :, None] == jnp.arange(capacity)[None, None, :]
    )
    expert_gate = jnp.sum(jnp.where(picked, gate_weights[:, :, None], 0.0), axis=1)
    outgoing = jnp.einsum(
        "poy,pj->oyj",
        placed_tokens.astype(jnp.bfloat16),
        normalized_input,
        preferred_element_type=jnp.float32,
    ).astype(jnp.bfloat16)
    combine_rows = (placed_tokens.astype(jnp.float32) * expert_gate[:, :, None]).reshape(
        count_of_tokens, experts * capacity
    )
    once_rows = outgoing.reshape(sections, expert_groups, capacity, width)
    arrived = lax.all_to_all(
        lax.all_to_all(once_rows, "sec", split_axis=0, concat_axis=0, tiled=True),
        "grp",
        split_axis=1,
        concat_axis=1,
        tiled=True,
    )
    local_rows = arrived.reshape(-1, width)
    every_out = expert_slice(
        lax.all_gather(local_rows, "tp", axis=0, tiled=True), expert_in, expert_out
    )
    own_sums = lax.psum_scatter(
        every_out.astype(jnp.float32).astype(jnp.bfloat16), "tp", scatter_dimension=0, tiled=True
    ).astype(jnp.float32)
    own_sums = own_sums.reshape(sections, expert_groups, capacity, width)
    back_rows = lax.all_to_all(
        lax.all_to_all(
            own_sums.astype(jnp.bfloat16), "grp", split_axis=1, concat_axis=1, tiled=True
        ),
        "sec",
        split_axis=0,
        concat_axis=0,
        tiled=True,
    ).astype(own_sums.dtype)
    expert_sums = back_rows.reshape(experts * capacity, width)
    expert_mix = jnp.dot(combine_rows, expert_sums, precision=lax.Precision.HIGHEST)
    return (residual + expert_mix).astype(jnp.bfloat16)


def solution(mesh):
    placed = (
        P(("sec", "grp", "tp"), None),
        P(("sec", "grp"), None, "tp", None),
        P(("sec", "grp"), None, None),
        P(("sec", "grp")),
        P(None, "tp", None, None),
        P(None, "tp", None, "grp"),
        P(),
        P(),
        P(("sec", "grp", "tp"), None),
        P(("sec", "grp", "tp")),
        P(("sec", "grp"), None, None, "tp"),
        P(("sec", "grp"), "tp", None),
    )
    body = shards_split if mesh.shape["tp"] > 1 else shards
    return jax.shard_map(
        body, mesh=mesh, in_specs=placed, out_specs=P(("sec", "grp", "tp"), None), check_vma=False
    )
```

```python
import functools

import jax
import jax.numpy as jnp
from jax import lax
from jax.experimental import pallas as pl
from jax.experimental.pallas import tpu as pltpu
from jax.sharding import PartitionSpec as P

score_scale = 192.0 ** (-0.5)
route_scale = 2.5


def divisor_at_most(number, most):
    return max(d for d in range(1, most + 1) if number % d == 0)


def project_kernel(heads_step, x_ref, w_ref, out_ref, total):
    step = pl.program_id(0)

    @pl.when(step == 0)
    def _():
        total[...] = jnp.zeros_like(total)

    value_width = w_ref.shape[2]
    part = jnp.zeros(total.shape, jnp.float32)
    pair = 2 if heads_step % 2 == 0 else 1
    for i in range(0, heads_step, pair):
        block = jnp.concatenate([w_ref[i + k] for k in range(pair)], axis=1)
        part += lax.dot_general(
            x_ref[:, i * value_width : (i + pair) * value_width],
            block,
            (((1,), (1,)), ((), ())),
            preferred_element_type=jnp.float32,
        )
    total[...] += part

    @pl.when(step == pl.num_programs(0) - 1)
    def _():
        out_ref[...] = total[...].astype(out_ref.dtype)


def project(rows, weight):
    heads, columns, value_width = weight.shape
    tokens = rows.shape[0]
    heads_step = divisor_at_most(heads, 8)
    return pl.pallas_call(
        functools.partial(project_kernel, heads_step),
        grid=(heads // heads_step,),
        in_specs=[
            pl.BlockSpec((tokens, heads_step * value_width), lambda i: (0, i)),
            pl.BlockSpec((heads_step, columns, value_width), lambda i: (i, 0, 0)),
        ],
        out_specs=pl.BlockSpec((tokens, columns), lambda i: (0, 0)),
        out_shape=jax.ShapeDtypeStruct((tokens, columns), jnp.float32),
        scratch_shapes=[pltpu.VMEM((tokens, columns), jnp.float32)],
        compiler_params=pltpu.CompilerParams(vmem_limit_bytes=16 * 1024 * 1024),
        cost_estimate=pl.CostEstimate(
            flops=2 * tokens * heads * value_width * columns,
            bytes_accessed=2 * heads * value_width * (columns + tokens),
            transcendentals=0,
        ),
        name="project",
    )(rows, weight)

MESH = pl.DeviceIdType.MESH


def flip(index, bit):
    return index + bit - 2 * bit * lax.rem(index // bit, 2)


def partner(bit):
    axis, value = bit
    return {axis: flip(lax.axis_index(axis), value)}


def greet(bits):
    barrier = pltpu.get_barrier_semaphore()
    for bit in bits:
        pl.semaphore_signal(barrier, inc=1, device_id=partner(bit), device_id_type=MESH)
    pl.semaphore_wait(barrier, len(bits))


def axis_bits(axis, size):
    return [(axis, 1 << k) for k in reversed(range(size.bit_length() - 1))]


def gather_kernel(orders, spans, flat, x_ref, out_ref, send_sems, recv_sems, own_sem):
    bits = orders[0]
    greet(bits)

    def block(subset, order):
        place = {axis: lax.axis_index(axis) for axis in flat}
        for k, (axis, value) in enumerate(order):
            if subset >> k & 1:
                place[axis] = flip(place[axis], value)
        index = 0
        for axis, size in flat.items():
            index = index * size + place[axis]
        return index

    def move(chunk, order, step, subset):
        first, count = spans[chunk]
        slot = out_ref.at[block(subset, order), pl.ds(first, count)]
        source = x_ref.at[pl.ds(first, count)] if subset == 0 else slot
        which = (1 << step) - 1 + subset
        return pltpu.make_async_remote_copy(
            src_ref=source,
            dst_ref=slot,
            send_sem=send_sems.at[chunk, which],
            recv_sem=recv_sems.at[chunk, which],
            device_id=partner(order[step]),
            device_id_type=MESH,
        )

    for step in range(len(bits)):
        for chunk, order in enumerate(orders):
            move(chunk, order, step, 0).start()
    own = pltpu.make_async_copy(x_ref, out_ref.at[block(0, bits)], own_sem)
    own.start()
    for step in range(len(bits)):
        for subset in range(1 << step):
            for chunk, order in enumerate(orders):
                move(chunk, order, step, subset).wait_recv()
                for later in range(step + 1, len(bits)):
                    move(chunk, order, later, subset + (1 << step)).start()
    for step in range(len(bits)):
        for subset in range(1 << step):
            for chunk, order in enumerate(orders):
                move(chunk, order, step, subset).wait_send()
    own.wait()


def gather(block, orders, flat, collective_id, name):
    rows, columns = block.shape
    blocks = 1
    for size in flat.values():
        blocks *= size
    count = rows // len(orders)
    spans = [(k * count, count) for k in range(len(orders))]
    return pl.pallas_call(
        functools.partial(gather_kernel, orders, spans, flat),
        out_shape=jax.ShapeDtypeStruct((blocks, rows, columns), block.dtype),
        in_specs=[pl.BlockSpec(memory_space=pltpu.VMEM)],
        out_specs=pl.BlockSpec(memory_space=pltpu.VMEM),
        scratch_shapes=[
            pltpu.SemaphoreType.DMA((len(orders), blocks - 1)),
            pltpu.SemaphoreType.DMA((len(orders), blocks - 1)),
            pltpu.SemaphoreType.DMA,
        ],
        compiler_params=pltpu.CompilerParams(
            collective_id=collective_id, has_side_effects=True, vmem_limit_bytes=40 * 1024 * 1024
        ),
        name=name,
    )(block)


def reduce_kernel(core, halving, whole_bits, orders, x_ref, out_ref, summed, from_core, half_in,
                  whole_in, core_sems, half_sems, whole_sems, end_sems):
    greet([core] + halving + whole_bits)
    groups, rows, width = x_ref.shape
    half = width // 2
    part = half // len(orders)
    side = lax.rem(lax.axis_index(core[0]) // core[1], 2)
    mine = pl.ds(pl.multiple_of(side * half, 128), half)
    other = pl.ds(pl.multiple_of((1 - side) * half, 128), half)
    my_bit = {bit: lax.rem(lax.axis_index(bit[0]) // bit[1], 2) for bit in halving}

    def group_of(done, current, sent, rest):
        index, place = 0, 0
        for bit in halving:
            if bit in done:
                value = my_bit[bit]
            elif bit == current:
                value = (1 - my_bit[bit]) if sent else my_bit[bit]
            else:
                value = rest >> place & 1
                place += 1
            index = index * 2 + value
        return index

    def remote(source, target, sems, device):
        return pltpu.make_async_remote_copy(
            src_ref=source, dst_ref=target, send_sem=sems.at[0], recv_sem=sems.at[1],
            device_id=partner(device), device_id_type=MESH,
        )

    def add(first, second):
        return (first.astype(jnp.float32) + second.astype(jnp.float32)).astype(jnp.bfloat16)

    pending = []
    firsts = [
        remote(x_ref.at[g, :, other], from_core.at[g], core_sems.at[g], core)
        for g in range(groups)
    ]
    for copy in firsts:
        copy.start()
    for g in range(groups):
        firsts[g].wait_recv()
        summed[g] = add(x_ref[g, :, mine], from_core[g])
    pending += firsts
    steps = len(halving)
    slots = [0]
    for step in range(steps):
        slots.append(slots[-1] + (1 << (steps - 1 - step)))

    def halve(step, chunk, rest):
        order = orders[chunk]
        span = pl.ds(chunk * part, part)
        slot = slots[step] + rest
        return remote(
            summed.at[group_of(order[:step], order[step], True, rest), :, span],
            half_in.at[slot, :, span],
            half_sems.at[chunk, slot],
            order[step],
        )

    for step in range(steps):
        for chunk in range(len(orders)):
            for rest in range(1 << (steps - 1 - step)):
                copy = halve(step, chunk, rest)
                copy.start()
                pending.append(copy)
        for chunk, order in enumerate(orders):
            span = pl.ds(chunk * part, part)
            for rest in range(1 << (steps - 1 - step)):
                halve(step, chunk, rest).wait_recv()
                g = group_of(order[:step], order[step], False, rest)
                summed[g, :, span] = add(
                    summed[g, :, span], half_in[slots[step] + rest, :, span]
                )
    group = group_of(halving, None, False, 0)
    current = summed[group]
    for k, bit in enumerate(whole_bits):
        whole_in[k, 0] = current
        copy = remote(whole_in.at[k, 0], whole_in.at[k, 1], whole_sems.at[k], bit)
        copy.start()
        copy.wait_recv()
        pending.append(copy)
        current = add(whole_in[k, 0], whole_in[k, 1])
    out_ref[:, mine] = current
    last = remote(out_ref.at[:, mine], out_ref.at[:, mine], end_sems, core)
    last.start()
    last.wait_recv()
    pending.append(last)
    for copy in pending:
        copy.wait_send()


def reduce_rows(values, core, halving, whole_bits, orders, collective_id):
    groups, rows, width = values.shape
    half = width // 2
    dma = pltpu.SemaphoreType.DMA
    return pl.pallas_call(
        functools.partial(reduce_kernel, core, halving, whole_bits, orders),
        out_shape=jax.ShapeDtypeStruct((rows, width), values.dtype),
        in_specs=[pl.BlockSpec(memory_space=pltpu.VMEM)],
        out_specs=pl.BlockSpec(memory_space=pltpu.VMEM),
        scratch_shapes=[
            pltpu.VMEM((groups, rows, half), jnp.bfloat16),
            pltpu.VMEM((groups, rows, half), jnp.bfloat16),
            pltpu.VMEM((groups - 1, rows, half), jnp.bfloat16),
            pltpu.VMEM((len(whole_bits), 2, rows, half), jnp.bfloat16),
            dma((groups, 2)),
            dma((len(orders), groups - 1, 2)),
            dma((len(whole_bits), 2)),
            dma((2,)),
        ],
        compiler_params=pltpu.CompilerParams(
            collective_id=collective_id, has_side_effects=True, vmem_limit_bytes=56 * 1024 * 1024
        ),
        name="reduce_rows",
    )(values)


def norm_kernel(columns, turn, x_ref, gain_ref, normed_ref, residual_ref, held):
    blocks, rows, _ = x_ref.shape
    width = gain_ref.shape[1]
    per = width // columns
    small = rows // len(turn)
    for section in range(blocks // per):
        span = pl.ds(section * rows, rows)
        squares = jnp.zeros((rows, 1), jnp.float32)
        for place in range(per):
            block = x_ref[section * per + place][:, :columns].astype(jnp.float32)
            block = jnp.concatenate([block[g * small : (g + 1) * small] for g in turn], axis=0)
            held[span, place * columns : (place + 1) * columns] = block
            squares += jnp.sum(block * block, axis=1, keepdims=True)
        scale = lax.rsqrt(squares / width + 1e-06)
        step = 512 if width % 512 == 0 else 128
        for first in range(0, width, step):
            part = held[span, first : first + step]
            residual_ref[span, first : first + step] = part.astype(jnp.bfloat16)
            normed_ref[span, first : first + step] = (
                part * scale * gain_ref[:, first : first + step]
            ).astype(jnp.bfloat16)


def norm_rows(gathered, gain, columns, turn):
    blocks, rows, _ = gathered.shape
    width = gain.shape[0]
    total = blocks * rows * columns // width
    vmem = pl.BlockSpec(memory_space=pltpu.VMEM)
    shape = jax.ShapeDtypeStruct((total, width), jnp.bfloat16)
    return pl.pallas_call(
        functools.partial(norm_kernel, columns, turn),
        out_shape=(shape, shape),
        in_specs=[vmem, vmem],
        out_specs=(vmem, vmem),
        scratch_shapes=[pltpu.VMEM((total, width), jnp.float32)],
        compiler_params=pltpu.CompilerParams(vmem_limit_bytes=32 * 1024 * 1024),
        name="norm_rows",
    )(gathered, gain[None, :])


def hidden_kernel(deep, x_ref, w_ref, out_ref, held, total, sems):
    depth = w_ref.shape[0]
    tiles = w_ref.shape[1]
    tokens = x_ref.shape[0]
    steps = depth // deep

    def fetch(step, slot):
        return [
            pltpu.make_async_copy(
                w_ref.at[pl.ds(step * deep, deep), tile], held.at[slot, tile], sems.at[slot, tile]
            )
            for tile in range(tiles)
        ]

    slots = held.shape[0]
    flat_held = held.reshape(slots, tiles, 2 * deep, 128)
    for ahead in range(slots - 1):
        for copy in fetch(ahead, ahead):
            copy.start()
    total[...] = jnp.zeros_like(total)
    row = lax.broadcasted_iota(jnp.int32, (128, 256), 0)
    column = lax.broadcasted_iota(jnp.int32, (128, 256), 1)
    even = (column == 2 * row).astype(jnp.bfloat16)
    odd = (column == 2 * row + 1).astype(jnp.bfloat16)

    def body(step, carry):
        slot = lax.rem(step, slots)

        @pl.when(step + slots - 1 < steps)
        def _():
            for copy in fetch(step + slots - 1, lax.rem(step + slots - 1, slots)):
                copy.start()

        for copy in fetch(step, slot):
            copy.wait()
        spread = []
        for k in range(deep // 128):
            first = pl.multiple_of(step * deep + k * 128, 128)
            x = x_ref[:, pl.ds(first, 128)]
            both = [
                jnp.dot(x, place, preferred_element_type=jnp.float32).astype(jnp.bfloat16)
                for place in (even, odd)
            ]
            spread.append(jnp.concatenate(both, axis=0))
        left = jnp.concatenate(spread, axis=1)
        for tile in range(0, tiles, 2):
            right = jnp.concatenate(
                [flat_held[slot, tile + j] for j in range(2)], axis=1
            )
            total[:, tile * 128 : tile * 128 + 256] += jnp.dot(
                left, right, preferred_element_type=jnp.float32
            )
        return carry

    lax.fori_loop(0, steps, body, 0)
    gate = total[:tokens, :]
    out_ref[...] = (gate / (1.0 + jnp.exp(-gate)) * total[tokens:, :]).astype(out_ref.dtype)


def hidden_units(rows, weight):
    depth, _, slice_width = weight.shape
    tokens = rows.shape[0]
    deep, slots = 256, 3
    tiles = slice_width // 128
    lanes = weight.reshape(depth, 2, tiles, 128).transpose(0, 2, 1, 3)
    return pl.pallas_call(
        functools.partial(hidden_kernel, deep),
        out_shape=jax.ShapeDtypeStruct((tokens, slice_width), jnp.bfloat16),
        in_specs=[pl.BlockSpec(memory_space=pltpu.VMEM), pl.BlockSpec(memory_space=pl.ANY)],
        out_specs=pl.BlockSpec(memory_space=pltpu.VMEM),
        scratch_shapes=[
            pltpu.VMEM((slots, tiles, deep, 2, 128), jnp.bfloat16),
            pltpu.VMEM((2 * tokens, slice_width), jnp.float32),
            pltpu.SemaphoreType.DMA((slots, tiles)),
        ],
        compiler_params=pltpu.CompilerParams(vmem_limit_bytes=40 * 1024 * 1024),
        name="hidden_units",
    )(rows, lanes)


def shards(
    hidden_in,
    queries,
    latent_cache,
    lengths,
    w_uv,
    attn_weight,
    norm_gain,
    router,
    routes,
    live_counts,
    expert_in,
    expert_out,
):
    own_tokens, width = hidden_in.shape
    sections = lax.axis_size("sec")
    expert_groups = lax.axis_size("grp")
    latent_width = w_uv.shape[2]
    experts = router.shape[1]

    tp = lax.axis_size("tp")
    grp_bits = axis_bits("grp", expert_groups)
    sec_bits = axis_bits("sec", sections)
    core, low, rest_bits = grp_bits[-1], grp_bits[-2], grp_bits[:-2]
    flat = {"sec": sections, "grp": expert_groups}

    picked = jnp.any(routes[:, :, None] == jnp.arange(experts)[None, None, :], axis=1)
    living = jnp.arange(own_tokens) < live_counts[0]
    unit_mask = (picked & living[:, None]).astype(jnp.bfloat16)
    unit_hidden = hidden_in
    if tp > 1:
        unit_mask = lax.all_gather(unit_mask, "tp", axis=0, tiled=True)
        unit_hidden = lax.all_gather(unit_hidden, "tp", axis=0, tiled=True)
    unit = unit_hidden.shape[0]
    hidden_part = lax.all_to_all(unit_hidden, "grp", split_axis=1, concat_axis=0, tiled=True)

    query_block = queries[:, :, 0, :]
    scores = (
        jnp.einsum("bhr,bpr->bhp", query_block, latent_cache, preferred_element_type=jnp.float32)
        * score_scale
    )
    positions = jnp.arange(latent_cache.shape[1])
    visible = positions[None, None, :] < lengths[:, None, None]
    scores = jnp.where(visible, scores, -1e30)
    highest = jnp.max(scores, axis=2, keepdims=True)
    raised = jnp.exp(scores - highest)
    softmax_weights = (raised / jnp.sum(raised, axis=2, keepdims=True)).astype(jnp.bfloat16)
    latent_out = jnp.einsum(
        "bhp,bpc->bhc",
        softmax_weights,
        latent_cache[:, :, :latent_width],
        preferred_element_type=jnp.float32,
    ).astype(jnp.bfloat16)
    head_out = jnp.einsum(
        "bhc,hcv->bhv", latent_out, w_uv[:, 0], preferred_element_type=jnp.float32
    ).astype(jnp.bfloat16)
    parts = max(1, 32 // unit)
    head_rows = head_out.reshape(unit, parts, -1).transpose(1, 0, 2).reshape(parts * unit, -1)
    group_blocks = gather(
        head_rows,
        [rest_bits + [low, core], [low] + rest_bits + [core]],
        {"grp": expert_groups},
        0,
        "gather_heads",
    )
    group_rows = (
        group_blocks.reshape(expert_groups, parts, unit, -1)
        .transpose(0, 2, 1, 3)
        .reshape(expert_groups * unit, -1)
    )
    column_part = project(group_rows, jnp.transpose(attn_weight[:, 0], (0, 2, 1)))
    if lax.axis_size("tp") > 1:
        column_part = lax.psum(column_part, "tp")
    column_part = column_part.astype(jnp.bfloat16).astype(jnp.float32)
    residual_part = (column_part + hidden_part.astype(jnp.float32)).astype(jnp.bfloat16)
    section_tokens, columns = residual_part.shape
    mask_block = jnp.pad(unit_mask, ((0, section_tokens - unit), (0, 0)))
    gathered = gather(
        jnp.concatenate([residual_part, mask_block], axis=1),
        [rest_bits + [low] + sec_bits + [core], sec_bits + [low] + rest_bits + [core]],
        flat,
        1,
        "gather_columns",
    )
    depth = len(grp_bits) - 1

    def reorder(rows):
        split = rows.reshape([sections] + [2] * depth + [2 * unit, rows.shape[-1]])
        turned = split.transpose([0] + list(range(depth, 0, -1)) + [depth + 1, depth + 2])
        return turned.reshape(-1, rows.shape[-1])

    mask_all = reorder(gathered[:, :unit, columns:].reshape(-1, experts)).astype(jnp.float32)
    turn = [
        sum(((g >> k) & 1) << (depth - 1 - k) for k in range(depth)) for g in range(1 << depth)
    ]
    normed, residual = norm_rows(gathered, norm_gain, columns, turn)
    affinity = jax.nn.sigmoid(jnp.dot(normed, router, preferred_element_type=jnp.float32))
    chosen = affinity * mask_all
    live_all = jnp.max(mask_all, axis=1, keepdims=True) > 0.0
    gate_all = jnp.where(
        live_all, route_scale * chosen / jnp.sum(chosen, axis=1, keepdims=True), 0.0
    )
    group = lax.axis_index("sec") * expert_groups + lax.axis_index("grp")
    own_gate = jnp.sum(
        jnp.where(jnp.arange(experts)[None, :] == group, gate_all, 0.0), axis=1, keepdims=True
    )

    activated = hidden_units(normed, expert_in[0])
    value = jnp.dot(activated, expert_out[0], preferred_element_type=jnp.float32)
    mixed = (value * own_gate).astype(jnp.bfloat16)
    grain = 4 * unit
    halving = sec_bits + [low] + list(reversed(rest_bits))[:-1]
    swapped = [low] + sec_bits + list(reversed(rest_bits))[:-1]
    mixed = mixed.reshape(-1, grain, width)
    shared = reduce_rows(mixed, core, halving, rest_bits[:1], [halving, swapped], 2)
    place = lax.axis_index("grp")
    quarter = (place // rest_bits[0][1]) % 2 * 2 + place % 2
    if tp > 1:
        owned = lax.dynamic_slice_in_dim(shared, quarter * unit, unit, 0)
        expert_mix = lax.psum_scatter(owned, "tp", scatter_dimension=0, tiled=True)
    else:
        expert_mix = lax.dynamic_slice_in_dim(shared, quarter * unit, unit, 0)
    own_row = 0
    for axis, value in halving + rest_bits[:1]:
        own_row = own_row * 2 + (lax.axis_index(axis) // value) % 2
    own_row = (own_row * 2 + place % 2) * unit + lax.axis_index("tp") * own_tokens
    own_residual = lax.dynamic_slice_in_dim(residual, own_row, own_tokens, 0).astype(jnp.float32)
    return (own_residual + expert_mix.astype(jnp.float32)).astype(jnp.bfloat16)


def expert_slice(rows_in, expert_in, expert_out):
    width = rows_in.shape[1]
    slice_width = expert_in.shape[3]
    gate_up = jnp.dot(
        rows_in, expert_in[0].reshape(width, 2 * slice_width), preferred_element_type=jnp.float32
    )
    activated = (jax.nn.silu(gate_up[:, :slice_width]) * gate_up[:, slice_width:]).astype(
        jnp.bfloat16
    )
    return jnp.dot(activated, expert_out[0], preferred_element_type=jnp.float32).astype(
        jnp.bfloat16
    )


def shards_split(
    hidden_in,
    queries,
    latent_cache,
    lengths,
    w_uv,
    attn_weight,
    norm_gain,
    router,
    routes,
    live_counts,
    expert_in,
    expert_out,
):
    count_of_tokens, width = hidden_in.shape
    sections = lax.axis_size("sec")
    expert_groups = lax.axis_size("grp")
    slices = lax.axis_size("tp")
    latent_width = w_uv.shape[2]
    query_block = queries[:, :, 0, :]
    scores = (
        jnp.einsum("bhr,bpr->bhp", query_block, latent_cache, preferred_element_type=jnp.float32)
        * score_scale
    )
    positions = jnp.arange(latent_cache.shape[1])
    visible = positions[None, None, :] < lengths[:, None, None]
    scores = jnp.where(visible, scores, -1e30)
    highest = jnp.max(scores, axis=2, keepdims=True)
    raised = jnp.exp(scores - highest)
    softmax_weights = (raised / jnp.sum(raised, axis=2, keepdims=True)).astype(jnp.bfloat16)
    latent_out = jnp.einsum(
        "bhp,bpc->bhc",
        softmax_weights,
        latent_cache[:, :, :latent_width],
        preferred_element_type=jnp.float32,
    ).astype(jnp.bfloat16)
    head_out = jnp.einsum(
        "bhc,hcv->bhv", latent_out, w_uv[:, 0], preferred_element_type=jnp.float32
    ).astype(jnp.bfloat16)
    head_rows = head_out.reshape(head_out.shape[0], -1)
    out_block = attn_weight[:, 0].reshape(-1, attn_weight.shape[3])
    partial_value = jnp.dot(
        lax.all_gather(head_rows, "grp", axis=0, tiled=True),
        out_block,
        preferred_element_type=jnp.float32,
    )
    partial_value = partial_value.reshape(
        expert_groups, slices, count_of_tokens, partial_value.shape[1]
    )
    summed = lax.psum_scatter(
        partial_value.astype(jnp.bfloat16), "tp", scatter_dimension=1, tiled=True
    ).astype(jnp.float32)
    column_part = summed[:, 0].astype(jnp.bfloat16)
    attention = lax.all_to_all(column_part, "grp", split_axis=0, concat_axis=2, tiled=True)[0]
    residual = hidden_in.astype(jnp.float32) + attention.astype(jnp.float32)
    normalized_input = (
        residual
        * lax.rsqrt(jnp.mean(residual * residual, axis=1, keepdims=True) + 1e-06)
        * norm_gain
    ).astype(jnp.bfloat16)
    experts = router.shape[1]
    per_token = routes.shape[1]
    capacity = max(2, 2 * count_of_tokens * per_token // experts)
    affinity = jax.nn.sigmoid(jnp.dot(normalized_input, router, preferred_element_type=jnp.float32))
    picked = routes[:, :, None] == jnp.arange(experts)[None, None, :]
    chosen = jnp.sum(jnp.where(picked, affinity[:, None, :], 0.0), axis=2)
    living = jnp.arange(count_of_tokens) < live_counts[0]
    gate_weights = (
        route_scale
        * chosen
        / jnp.sum(chosen, axis=1, keepdims=True)
        * living[:, None].astype(jnp.float32)
    )
    routed = jnp.any(picked, axis=1) & living[:, None]
    routed_count = routed.astype(jnp.int32)
    slot_index = jnp.cumsum(routed_count, axis=0) - routed_count
    placed_tokens = routed[:, :, None] & (
        slot_index[:, :, None] == jnp.arange(capacity)[None, None, :]
    )
    expert_gate = jnp.sum(jnp.where(picked, gate_weights[:, :, None], 0.0), axis=1)
    outgoing = jnp.einsum(
        "poy,pj->oyj",
        placed_tokens.astype(jnp.bfloat16),
        normalized_input,
        preferred_element_type=jnp.float32,
    ).astype(jnp.bfloat16)
    combine_rows = (placed_tokens.astype(jnp.float32) * expert_gate[:, :, None]).reshape(
        count_of_tokens, experts * capacity
    )
    once_rows = outgoing.reshape(sections, expert_groups, capacity, width)
    arrived = lax.all_to_all(
        lax.all_to_all(once_rows, "sec", split_axis=0, concat_axis=0, tiled=True),
        "grp",
        split_axis=1,
        concat_axis=1,
        tiled=True,
    )
    local_rows = arrived.reshape(-1, width)
    every_out = expert_slice(
        lax.all_gather(local_rows, "tp", axis=0, tiled=True), expert_in, expert_out
    )
    own_sums = lax.psum_scatter(
        every_out.astype(jnp.float32).astype(jnp.bfloat16), "tp", scatter_dimension=0, tiled=True
    ).astype(jnp.float32)
    own_sums = own_sums.reshape(sections, expert_groups, capacity, width)
    back_rows = lax.all_to_all(
        lax.all_to_all(
            own_sums.astype(jnp.bfloat16), "grp", split_axis=1, concat_axis=1, tiled=True
        ),
        "sec",
        split_axis=0,
        concat_axis=0,
        tiled=True,
    ).astype(own_sums.dtype)
    expert_sums = back_rows.reshape(experts * capacity, width)
    expert_mix = jnp.dot(combine_rows, expert_sums, precision=lax.Precision.HIGHEST)
    return (residual + expert_mix).astype(jnp.bfloat16)


def solution(mesh):
    placed = (
        P(("sec", "grp", "tp"), None),
        P(("sec", "grp"), None, "tp", None),
        P(("sec", "grp"), None, None),
        P(("sec", "grp")),
        P(None, "tp", None, None),
        P(None, "tp", None, "grp"),
        P(),
        P(),
        P(("sec", "grp", "tp"), None),
        P(("sec", "grp", "tp")),
        P(("sec", "grp"), None, None, "tp"),
        P(("sec", "grp"), "tp", None),
    )
    body = shards_split if mesh.shape["tp"] > 1 else shards
    return jax.shard_map(
        body, mesh=mesh, in_specs=placed, out_specs=P(("sec", "grp", "tp"), None), check_vma=False
    )
```

```python
import functools

import jax
import jax.numpy as jnp
from jax import lax
from jax.experimental import pallas as pl
from jax.experimental.pallas import tpu as pltpu
from jax.sharding import PartitionSpec as P

score_scale = 192.0 ** (-0.5)
route_scale = 2.5


def divisor_at_most(number, most):
    return max(d for d in range(1, most + 1) if number % d == 0)


def project_kernel(heads_step, x_ref, w_ref, out_ref, total):
    step = pl.program_id(0)

    @pl.when(step == 0)
    def _():
        total[...] = jnp.zeros_like(total)

    value_width = w_ref.shape[2]
    part = jnp.zeros(total.shape, jnp.float32)
    pair = 2 if heads_step % 2 == 0 else 1
    for i in range(0, heads_step, pair):
        block = jnp.concatenate([w_ref[i + k] for k in range(pair)], axis=1)
        part += lax.dot_general(
            x_ref[:, i * value_width : (i + pair) * value_width],
            block,
            (((1,), (1,)), ((), ())),
            preferred_element_type=jnp.float32,
        )
    total[...] += part

    @pl.when(step == pl.num_programs(0) - 1)
    def _():
        out_ref[...] = total[...].astype(out_ref.dtype)


def project(rows, weight):
    heads, columns, value_width = weight.shape
    tokens = rows.shape[0]
    heads_step = divisor_at_most(heads, 8)
    return pl.pallas_call(
        functools.partial(project_kernel, heads_step),
        grid=(heads // heads_step,),
        in_specs=[
            pl.BlockSpec((tokens, heads_step * value_width), lambda i: (0, i)),
            pl.BlockSpec((heads_step, columns, value_width), lambda i: (i, 0, 0)),
        ],
        out_specs=pl.BlockSpec((tokens, columns), lambda i: (0, 0)),
        out_shape=jax.ShapeDtypeStruct((tokens, columns), jnp.float32),
        scratch_shapes=[pltpu.VMEM((tokens, columns), jnp.float32)],
        compiler_params=pltpu.CompilerParams(vmem_limit_bytes=56 * 1024 * 1024),
        cost_estimate=pl.CostEstimate(
            flops=2 * tokens * heads * value_width * columns,
            bytes_accessed=2 * heads * value_width * (columns + tokens),
            transcendentals=0,
        ),
        name="project",
    )(rows, weight)

MESH = pl.DeviceIdType.MESH


def flip(index, bit):
    return index + bit - 2 * bit * lax.rem(index // bit, 2)


def partner(bit):
    axis, value = bit
    return {axis: flip(lax.axis_index(axis), value)}


def greet(bits):
    barrier = pltpu.get_barrier_semaphore()
    for bit in bits:
        pl.semaphore_signal(barrier, inc=1, device_id=partner(bit), device_id_type=MESH)
    pl.semaphore_wait(barrier, len(bits))


def axis_bits(axis, size):
    return [(axis, 1 << k) for k in reversed(range(size.bit_length() - 1))]


def gather_kernel(orders, spans, flat, x_ref, out_ref, send_sems, recv_sems, own_sem):
    bits = orders[0]
    greet(bits)

    def block(subset, order):
        place = {axis: lax.axis_index(axis) for axis in flat}
        for k, (axis, value) in enumerate(order):
            if subset >> k & 1:
                place[axis] = flip(place[axis], value)
        index = 0
        for axis, size in flat.items():
            index = index * size + place[axis]
        return index

    def move(chunk, order, step, subset):
        first, count = spans[chunk]
        slot = out_ref.at[block(subset, order), pl.ds(first, count)]
        source = x_ref.at[pl.ds(first, count)] if subset == 0 else slot
        which = (1 << step) - 1 + subset
        return pltpu.make_async_remote_copy(
            src_ref=source,
            dst_ref=slot,
            send_sem=send_sems.at[chunk, which],
            recv_sem=recv_sems.at[chunk, which],
            device_id=partner(order[step]),
            device_id_type=MESH,
        )

    for step in range(len(bits)):
        for chunk, order in enumerate(orders):
            move(chunk, order, step, 0).start()
    own = pltpu.make_async_copy(x_ref, out_ref.at[block(0, bits)], own_sem)
    own.start()
    for step in range(len(bits)):
        for subset in range(1 << step):
            for chunk, order in enumerate(orders):
                move(chunk, order, step, subset).wait_recv()
                for later in range(step + 1, len(bits)):
                    move(chunk, order, later, subset + (1 << step)).start()
    for step in range(len(bits)):
        for subset in range(1 << step):
            for chunk, order in enumerate(orders):
                move(chunk, order, step, subset).wait_send()
    own.wait()


def gather(block, orders, flat, collective_id, name):
    rows, columns = block.shape
    blocks = 1
    for size in flat.values():
        blocks *= size
    count = rows // len(orders)
    spans = [(k * count, count) for k in range(len(orders))]
    return pl.pallas_call(
        functools.partial(gather_kernel, orders, spans, flat),
        out_shape=jax.ShapeDtypeStruct((blocks, rows, columns), block.dtype),
        in_specs=[pl.BlockSpec(memory_space=pltpu.VMEM)],
        out_specs=pl.BlockSpec(memory_space=pltpu.VMEM),
        scratch_shapes=[
            pltpu.SemaphoreType.DMA((len(orders), blocks - 1)),
            pltpu.SemaphoreType.DMA((len(orders), blocks - 1)),
            pltpu.SemaphoreType.DMA,
        ],
        compiler_params=pltpu.CompilerParams(
            collective_id=collective_id, has_side_effects=True, vmem_limit_bytes=40 * 1024 * 1024
        ),
        name=name,
    )(block)


def reduce_kernel(core, halving, whole_bits, orders, x_ref, out_ref, summed, from_core, half_in,
                  whole_in, core_sems, half_sems, whole_sems, end_sems):
    greet([core] + halving + whole_bits)
    groups, rows, width = x_ref.shape
    half = width // 2
    part = half // len(orders)
    side = lax.rem(lax.axis_index(core[0]) // core[1], 2)
    mine = pl.ds(pl.multiple_of(side * half, 128), half)
    other = pl.ds(pl.multiple_of((1 - side) * half, 128), half)
    my_bit = {bit: lax.rem(lax.axis_index(bit[0]) // bit[1], 2) for bit in halving}

    def group_of(done, current, sent, rest):
        index, place = 0, 0
        for bit in halving:
            if bit in done:
                value = my_bit[bit]
            elif bit == current:
                value = (1 - my_bit[bit]) if sent else my_bit[bit]
            else:
                value = rest >> place & 1
                place += 1
            index = index * 2 + value
        return index

    def remote(source, target, sems, device):
        return pltpu.make_async_remote_copy(
            src_ref=source, dst_ref=target, send_sem=sems.at[0], recv_sem=sems.at[1],
            device_id=partner(device), device_id_type=MESH,
        )

    def add(first, second):
        return (first.astype(jnp.float32) + second.astype(jnp.float32)).astype(jnp.bfloat16)

    pending = []
    firsts = [
        remote(x_ref.at[g, :, other], from_core.at[g], core_sems.at[g], core)
        for g in range(groups)
    ]
    for copy in firsts:
        copy.start()
    for g in range(groups):
        firsts[g].wait_recv()
        summed[g] = add(x_ref[g, :, mine], from_core[g])
    pending += firsts
    steps = len(halving)
    slots = [0]
    for step in range(steps):
        slots.append(slots[-1] + (1 << (steps - 1 - step)))

    def halve(step, chunk, rest):
        order = orders[chunk]
        span = pl.ds(chunk * part, part)
        slot = slots[step] + rest
        return remote(
            summed.at[group_of(order[:step], order[step], True, rest), :, span],
            half_in.at[slot, :, span],
            half_sems.at[chunk, slot],
            order[step],
        )

    for step in range(steps):
        for chunk in range(len(orders)):
            for rest in range(1 << (steps - 1 - step)):
                copy = halve(step, chunk, rest)
                copy.start()
                pending.append(copy)
        for chunk, order in enumerate(orders):
            span = pl.ds(chunk * part, part)
            for rest in range(1 << (steps - 1 - step)):
                halve(step, chunk, rest).wait_recv()
                g = group_of(order[:step], order[step], False, rest)
                summed[g, :, span] = add(
                    summed[g, :, span], half_in[slots[step] + rest, :, span]
                )
    group = group_of(halving, None, False, 0)
    current = summed[group]
    for k, bit in enumerate(whole_bits):
        whole_in[k, 0] = current
        copy = remote(whole_in.at[k, 0], whole_in.at[k, 1], whole_sems.at[k], bit)
        copy.start()
        copy.wait_recv()
        pending.append(copy)
        current = add(whole_in[k, 0], whole_in[k, 1])
    out_ref[:, mine] = current
    last = remote(out_ref.at[:, mine], out_ref.at[:, mine], end_sems, core)
    last.start()
    last.wait_recv()
    pending.append(last)
    for copy in pending:
        copy.wait_send()


def reduce_rows(values, core, halving, whole_bits, orders, collective_id):
    groups, rows, width = values.shape
    half = width // 2
    dma = pltpu.SemaphoreType.DMA
    return pl.pallas_call(
        functools.partial(reduce_kernel, core, halving, whole_bits, orders),
        out_shape=jax.ShapeDtypeStruct((rows, width), values.dtype),
        in_specs=[pl.BlockSpec(memory_space=pltpu.VMEM)],
        out_specs=pl.BlockSpec(memory_space=pltpu.VMEM),
        scratch_shapes=[
            pltpu.VMEM((groups, rows, half), jnp.bfloat16),
            pltpu.VMEM((groups, rows, half), jnp.bfloat16),
            pltpu.VMEM((groups - 1, rows, half), jnp.bfloat16),
            pltpu.VMEM((len(whole_bits), 2, rows, half), jnp.bfloat16),
            dma((groups, 2)),
            dma((len(orders), groups - 1, 2)),
            dma((len(whole_bits), 2)),
            dma((2,)),
        ],
        compiler_params=pltpu.CompilerParams(
            collective_id=collective_id, has_side_effects=True, vmem_limit_bytes=56 * 1024 * 1024
        ),
        name="reduce_rows",
    )(values)


def norm_kernel(columns, turn, x_ref, gain_ref, normed_ref, residual_ref, held):
    blocks, rows, _ = x_ref.shape
    width = gain_ref.shape[1]
    per = width // columns
    small = rows // len(turn)
    for section in range(blocks // per):
        span = pl.ds(section * rows, rows)
        squares = jnp.zeros((rows, 1), jnp.float32)
        for place in range(per):
            block = x_ref[section * per + place][:, :columns].astype(jnp.float32)
            block = jnp.concatenate([block[g * small : (g + 1) * small] for g in turn], axis=0)
            held[span, place * columns : (place + 1) * columns] = block
            squares += jnp.sum(block * block, axis=1, keepdims=True)
        scale = lax.rsqrt(squares / width + 1e-06)
        step = 512 if width % 512 == 0 else 128
        for first in range(0, width, step):
            part = held[span, first : first + step]
            residual_ref[span, first : first + step] = part.astype(jnp.bfloat16)
            normed_ref[span, first : first + step] = (
                part * scale * gain_ref[:, first : first + step]
            ).astype(jnp.bfloat16)


def norm_rows(gathered, gain, columns, turn):
    blocks, rows, _ = gathered.shape
    width = gain.shape[0]
    total = blocks * rows * columns // width
    vmem = pl.BlockSpec(memory_space=pltpu.VMEM)
    shape = jax.ShapeDtypeStruct((total, width), jnp.bfloat16)
    return pl.pallas_call(
        functools.partial(norm_kernel, columns, turn),
        out_shape=(shape, shape),
        in_specs=[vmem, vmem],
        out_specs=(vmem, vmem),
        scratch_shapes=[pltpu.VMEM((total, width), jnp.float32)],
        compiler_params=pltpu.CompilerParams(vmem_limit_bytes=32 * 1024 * 1024),
        name="norm_rows",
    )(gathered, gain[None, :])


def hidden_kernel(deep, x_ref, w_ref, out_ref, held, total, sems):
    depth = w_ref.shape[0]
    tiles = w_ref.shape[1]
    tokens = x_ref.shape[0]
    steps = depth // deep

    def fetch(step, slot):
        return [
            pltpu.make_async_copy(
                w_ref.at[pl.ds(step * deep, deep), tile], held.at[slot, tile], sems.at[slot, tile]
            )
            for tile in range(tiles)
        ]

    slots = held.shape[0]
    flat_held = held.reshape(slots, tiles, 2 * deep, 128)
    for ahead in range(slots - 1):
        for copy in fetch(ahead, ahead):
            copy.start()
    total[...] = jnp.zeros_like(total)
    row = lax.broadcasted_iota(jnp.int32, (128, 256), 0)
    column = lax.broadcasted_iota(jnp.int32, (128, 256), 1)
    even = (column == 2 * row).astype(jnp.bfloat16)
    odd = (column == 2 * row + 1).astype(jnp.bfloat16)

    def body(step, carry):
        slot = lax.rem(step, slots)

        @pl.when(step + slots - 1 < steps)
        def _():
            for copy in fetch(step + slots - 1, lax.rem(step + slots - 1, slots)):
                copy.start()

        for copy in fetch(step, slot):
            copy.wait()
        spread = []
        for k in range(deep // 128):
            first = pl.multiple_of(step * deep + k * 128, 128)
            x = x_ref[:, pl.ds(first, 128)]
            both = [
                jnp.dot(x, place, preferred_element_type=jnp.float32).astype(jnp.bfloat16)
                for place in (even, odd)
            ]
            spread.append(jnp.concatenate(both, axis=0))
        left = jnp.concatenate(spread, axis=1)
        for tile in range(0, tiles, 2):
            right = jnp.concatenate(
                [flat_held[slot, tile + j] for j in range(2)], axis=1
            )
            total[:, tile * 128 : tile * 128 + 256] += jnp.dot(
                left, right, preferred_element_type=jnp.float32
            )
        return carry

    lax.fori_loop(0, steps, body, 0)
    gate = total[:tokens, :]
    out_ref[...] = (gate / (1.0 + jnp.exp(-gate)) * total[tokens:, :]).astype(out_ref.dtype)


def hidden_units(rows, weight):
    depth, _, slice_width = weight.shape
    tokens = rows.shape[0]
    deep, slots = 256, 8
    tiles = slice_width // 128
    lanes = weight.reshape(depth, 2, tiles, 128).transpose(0, 2, 1, 3)
    return pl.pallas_call(
        functools.partial(hidden_kernel, deep),
        out_shape=jax.ShapeDtypeStruct((tokens, slice_width), jnp.bfloat16),
        in_specs=[pl.BlockSpec(memory_space=pltpu.VMEM), pl.BlockSpec(memory_space=pl.ANY)],
        out_specs=pl.BlockSpec(memory_space=pltpu.VMEM),
        scratch_shapes=[
            pltpu.VMEM((slots, tiles, deep, 2, 128), jnp.bfloat16),
            pltpu.VMEM((2 * tokens, slice_width), jnp.float32),
            pltpu.SemaphoreType.DMA((slots, tiles)),
        ],
        compiler_params=pltpu.CompilerParams(vmem_limit_bytes=40 * 1024 * 1024),
        name="hidden_units",
    )(rows, lanes)


def shards(
    hidden_in,
    queries,
    latent_cache,
    lengths,
    w_uv,
    attn_weight,
    norm_gain,
    router,
    routes,
    live_counts,
    expert_in,
    expert_out,
):
    own_tokens, width = hidden_in.shape
    sections = lax.axis_size("sec")
    expert_groups = lax.axis_size("grp")
    latent_width = w_uv.shape[2]
    experts = router.shape[1]

    tp = lax.axis_size("tp")
    grp_bits = axis_bits("grp", expert_groups)
    sec_bits = axis_bits("sec", sections)
    core, low, rest_bits = grp_bits[-1], grp_bits[-2], grp_bits[:-2]
    flat = {"sec": sections, "grp": expert_groups}

    picked = jnp.any(routes[:, :, None] == jnp.arange(experts)[None, None, :], axis=1)
    living = jnp.arange(own_tokens) < live_counts[0]
    unit_mask = (picked & living[:, None]).astype(jnp.bfloat16)
    unit_hidden = hidden_in
    if tp > 1:
        unit_mask = lax.all_gather(unit_mask, "tp", axis=0, tiled=True)
        unit_hidden = lax.all_gather(unit_hidden, "tp", axis=0, tiled=True)
    unit = unit_hidden.shape[0]
    hidden_part = lax.all_to_all(unit_hidden, "grp", split_axis=1, concat_axis=0, tiled=True)

    query_block = queries[:, :, 0, :]
    scores = (
        jnp.einsum("bhr,bpr->bhp", query_block, latent_cache, preferred_element_type=jnp.float32)
        * score_scale
    )
    positions = jnp.arange(latent_cache.shape[1])
    visible = positions[None, None, :] < lengths[:, None, None]
    scores = jnp.where(visible, scores, -1e30)
    highest = jnp.max(scores, axis=2, keepdims=True)
    raised = jnp.exp(scores - highest)
    softmax_weights = (raised / jnp.sum(raised, axis=2, keepdims=True)).astype(jnp.bfloat16)
    latent_out = jnp.einsum(
        "bhp,bpc->bhc",
        softmax_weights,
        latent_cache[:, :, :latent_width],
        preferred_element_type=jnp.float32,
    ).astype(jnp.bfloat16)
    head_out = jnp.einsum(
        "bhc,hcv->bhv", latent_out, w_uv[:, 0], preferred_element_type=jnp.float32
    ).astype(jnp.bfloat16)
    parts = max(1, 32 // unit)
    head_rows = head_out.reshape(unit, parts, -1).transpose(1, 0, 2).reshape(parts * unit, -1)
    group_blocks = gather(
        head_rows,
        [rest_bits + [low, core], [low] + rest_bits + [core]],
        {"grp": expert_groups},
        0,
        "gather_heads",
    )
    group_rows = (
        group_blocks.reshape(expert_groups, parts, unit, -1)
        .transpose(0, 2, 1, 3)
        .reshape(expert_groups * unit, -1)
    )
    column_part = project(group_rows, jnp.transpose(attn_weight[:, 0], (0, 2, 1)))
    if lax.axis_size("tp") > 1:
        column_part = lax.psum(column_part, "tp")
    column_part = column_part.astype(jnp.bfloat16).astype(jnp.float32)
    residual_part = (column_part + hidden_part.astype(jnp.float32)).astype(jnp.bfloat16)
    section_tokens, columns = residual_part.shape
    mask_block = jnp.pad(unit_mask, ((0, section_tokens - unit), (0, 0)))
    gathered = gather(
        jnp.concatenate([residual_part, mask_block], axis=1),
        [rest_bits + [low] + sec_bits + [core], sec_bits + [low] + rest_bits + [core]],
        flat,
        1,
        "gather_columns",
    )
    depth = len(grp_bits) - 1

    def reorder(rows):
        split = rows.reshape([sections] + [2] * depth + [2 * unit, rows.shape[-1]])
        turned = split.transpose([0] + list(range(depth, 0, -1)) + [depth + 1, depth + 2])
        return turned.reshape(-1, rows.shape[-1])

    mask_all = reorder(gathered[:, :unit, columns:].reshape(-1, experts)).astype(jnp.float32)
    turn = [
        sum(((g >> k) & 1) << (depth - 1 - k) for k in range(depth)) for g in range(1 << depth)
    ]
    normed, residual = norm_rows(gathered, norm_gain, columns, turn)
    affinity = jax.nn.sigmoid(jnp.dot(normed, router, preferred_element_type=jnp.float32))
    chosen = affinity * mask_all
    live_all = jnp.max(mask_all, axis=1, keepdims=True) > 0.0
    gate_all = jnp.where(
        live_all, route_scale * chosen / jnp.sum(chosen, axis=1, keepdims=True), 0.0
    )
    group = lax.axis_index("sec") * expert_groups + lax.axis_index("grp")
    own_gate = jnp.sum(
        jnp.where(jnp.arange(experts)[None, :] == group, gate_all, 0.0), axis=1, keepdims=True
    )

    activated = hidden_units(normed, expert_in[0])
    value = jnp.dot(activated, expert_out[0], preferred_element_type=jnp.float32)
    mixed = (value * own_gate).astype(jnp.bfloat16)
    grain = 4 * unit
    halving = sec_bits + [low] + list(reversed(rest_bits))[:-1]
    swapped = [low] + sec_bits + list(reversed(rest_bits))[:-1]
    mixed = mixed.reshape(-1, grain, width)
    shared = reduce_rows(mixed, core, halving, rest_bits[:1], [halving, swapped], 2)
    place = lax.axis_index("grp")
    quarter = (place // rest_bits[0][1]) % 2 * 2 + place % 2
    if tp > 1:
        owned = lax.dynamic_slice_in_dim(shared, quarter * unit, unit, 0)
        expert_mix = lax.psum_scatter(owned, "tp", scatter_dimension=0, tiled=True)
    else:
        expert_mix = lax.dynamic_slice_in_dim(shared, quarter * unit, unit, 0)
    own_row = 0
    for axis, value in halving + rest_bits[:1]:
        own_row = own_row * 2 + (lax.axis_index(axis) // value) % 2
    own_row = (own_row * 2 + place % 2) * unit + lax.axis_index("tp") * own_tokens
    own_residual = lax.dynamic_slice_in_dim(residual, own_row, own_tokens, 0).astype(jnp.float32)
    return (own_residual + expert_mix.astype(jnp.float32)).astype(jnp.bfloat16)


def expert_slice(rows_in, expert_in, expert_out):
    width = rows_in.shape[1]
    slice_width = expert_in.shape[3]
    gate_up = jnp.dot(
        rows_in, expert_in[0].reshape(width, 2 * slice_width), preferred_element_type=jnp.float32
    )
    activated = (jax.nn.silu(gate_up[:, :slice_width]) * gate_up[:, slice_width:]).astype(
        jnp.bfloat16
    )
    return jnp.dot(activated, expert_out[0], preferred_element_type=jnp.float32).astype(
        jnp.bfloat16
    )


def shards_split(
    hidden_in,
    queries,
    latent_cache,
    lengths,
    w_uv,
    attn_weight,
    norm_gain,
    router,
    routes,
    live_counts,
    expert_in,
    expert_out,
):
    count_of_tokens, width = hidden_in.shape
    sections = lax.axis_size("sec")
    expert_groups = lax.axis_size("grp")
    slices = lax.axis_size("tp")
    latent_width = w_uv.shape[2]
    query_block = queries[:, :, 0, :]
    scores = (
        jnp.einsum("bhr,bpr->bhp", query_block, latent_cache, preferred_element_type=jnp.float32)
        * score_scale
    )
    positions = jnp.arange(latent_cache.shape[1])
    visible = positions[None, None, :] < lengths[:, None, None]
    scores = jnp.where(visible, scores, -1e30)
    highest = jnp.max(scores, axis=2, keepdims=True)
    raised = jnp.exp(scores - highest)
    softmax_weights = (raised / jnp.sum(raised, axis=2, keepdims=True)).astype(jnp.bfloat16)
    latent_out = jnp.einsum(
        "bhp,bpc->bhc",
        softmax_weights,
        latent_cache[:, :, :latent_width],
        preferred_element_type=jnp.float32,
    ).astype(jnp.bfloat16)
    head_out = jnp.einsum(
        "bhc,hcv->bhv", latent_out, w_uv[:, 0], preferred_element_type=jnp.float32
    ).astype(jnp.bfloat16)
    head_rows = head_out.reshape(head_out.shape[0], -1)
    out_block = attn_weight[:, 0].reshape(-1, attn_weight.shape[3])
    partial_value = jnp.dot(
        lax.all_gather(head_rows, "grp", axis=0, tiled=True),
        out_block,
        preferred_element_type=jnp.float32,
    )
    partial_value = partial_value.reshape(
        expert_groups, slices, count_of_tokens, partial_value.shape[1]
    )
    summed = lax.psum_scatter(
        partial_value.astype(jnp.bfloat16), "tp", scatter_dimension=1, tiled=True
    ).astype(jnp.float32)
    column_part = summed[:, 0].astype(jnp.bfloat16)
    attention = lax.all_to_all(column_part, "grp", split_axis=0, concat_axis=2, tiled=True)[0]
    residual = hidden_in.astype(jnp.float32) + attention.astype(jnp.float32)
    normalized_input = (
        residual
        * lax.rsqrt(jnp.mean(residual * residual, axis=1, keepdims=True) + 1e-06)
        * norm_gain
    ).astype(jnp.bfloat16)
    experts = router.shape[1]
    per_token = routes.shape[1]
    capacity = max(2, 2 * count_of_tokens * per_token // experts)
    affinity = jax.nn.sigmoid(jnp.dot(normalized_input, router, preferred_element_type=jnp.float32))
    picked = routes[:, :, None] == jnp.arange(experts)[None, None, :]
    chosen = jnp.sum(jnp.where(picked, affinity[:, None, :], 0.0), axis=2)
    living = jnp.arange(count_of_tokens) < live_counts[0]
    gate_weights = (
        route_scale
        * chosen
        / jnp.sum(chosen, axis=1, keepdims=True)
        * living[:, None].astype(jnp.float32)
    )
    routed = jnp.any(picked, axis=1) & living[:, None]
    routed_count = routed.astype(jnp.int32)
    slot_index = jnp.cumsum(routed_count, axis=0) - routed_count
    placed_tokens = routed[:, :, None] & (
        slot_index[:, :, None] == jnp.arange(capacity)[None, None, :]
    )
    expert_gate = jnp.sum(jnp.where(picked, gate_weights[:, :, None], 0.0), axis=1)
    outgoing = jnp.einsum(
        "poy,pj->oyj",
        placed_tokens.astype(jnp.bfloat16),
        normalized_input,
        preferred_element_type=jnp.float32,
    ).astype(jnp.bfloat16)
    combine_rows = (placed_tokens.astype(jnp.float32) * expert_gate[:, :, None]).reshape(
        count_of_tokens, experts * capacity
    )
    once_rows = outgoing.reshape(sections, expert_groups, capacity, width)
    arrived = lax.all_to_all(
        lax.all_to_all(once_rows, "sec", split_axis=0, concat_axis=0, tiled=True),
        "grp",
        split_axis=1,
        concat_axis=1,
        tiled=True,
    )
    local_rows = arrived.reshape(-1, width)
    every_out = expert_slice(
        lax.all_gather(local_rows, "tp", axis=0, tiled=True), expert_in, expert_out
    )
    own_sums = lax.psum_scatter(
        every_out.astype(jnp.float32).astype(jnp.bfloat16), "tp", scatter_dimension=0, tiled=True
    ).astype(jnp.float32)
    own_sums = own_sums.reshape(sections, expert_groups, capacity, width)
    back_rows = lax.all_to_all(
        lax.all_to_all(
            own_sums.astype(jnp.bfloat16), "grp", split_axis=1, concat_axis=1, tiled=True
        ),
        "sec",
        split_axis=0,
        concat_axis=0,
        tiled=True,
    ).astype(own_sums.dtype)
    expert_sums = back_rows.reshape(experts * capacity, width)
    expert_mix = jnp.dot(combine_rows, expert_sums, precision=lax.Precision.HIGHEST)
    return (residual + expert_mix).astype(jnp.bfloat16)


def solution(mesh):
    placed = (
        P(("sec", "grp", "tp"), None),
        P(("sec", "grp"), None, "tp", None),
        P(("sec", "grp"), None, None),
        P(("sec", "grp")),
        P(None, "tp", None, None),
        P(None, "tp", None, "grp"),
        P(),
        P(),
        P(("sec", "grp", "tp"), None),
        P(("sec", "grp", "tp")),
        P(("sec", "grp"), None, None, "tp"),
        P(("sec", "grp"), "tp", None),
    )
    body = shards_split if mesh.shape["tp"] > 1 else shards
    return jax.shard_map(
        body, mesh=mesh, in_specs=placed, out_specs=P(("sec", "grp", "tp"), None), check_vma=False
    )
```
